32 devices in a mesh: ctx: 4 (over y, x), exp: 8 (over z, core).
Axes of the slice: x: 2, y: 2, z: 4, core: 2. Of those that a mesh axis runs over, the one named last changes fastest.
Arguments:
- tokens: bfloat16 [1024, 7168], P('exp', 'ctx'), may hold values from -6 to 6
- cotangent: bfloat16 [1024, 7168], P('exp', 'ctx'), may hold values from -6 to 6
- routes: int32 [1024, 8], P('exp'), may hold values from 0 to 255, all different within a row; in each aligned block of 128 rows (0 to 127, 128 to 255, ...) at most 6 rows name the same one
- gate_weights: float32 [1024, 8], P('exp'), may hold values from 0.1 to 0.7
- w_gate: bfloat16 [8, 7168, 1024], P('exp', 'ctx'), may hold values from -0.0625 to 0.0625
- w_up: bfloat16 [8, 7168, 1024], P('exp', 'ctx'), may hold values from -0.0625 to 0.0625
- w_down: bfloat16 [8, 1024, 7168], P('exp', None, 'ctx'), may hold values from -0.1875 to 0.1875
Outputs:
- combined: bfloat16 [1024, 7168], P('exp', 'ctx')
- d_tokens: bfloat16 [1024, 7168], P('exp', 'ctx')
- d_gate: bfloat16 [8, 7168, 1024], P('exp', 'ctx')
- d_up: bfloat16 [8, 7168, 1024], P('exp', 'ctx')
- d_down: bfloat16 [8, 1024, 7168], P('exp', None, 'ctx')
The draws below stay inside these ranges and needn't reach their ends.
Inputs may be any that keep to these rules, and one draw needn't show every extreme that they name: The 8 routes of a token are distinct. Within each aligned block of 128 tokens no expert is named by more than 6 tokens, a bound that some block reaches.
All inputs are finite; a program needn't handle non-finite values.
Results may differ from the reference program's by a relative error of at most 0.0066.
Values may be sent and summed in bfloat16 or wider, within the bound.
A program may use at most 64 MiB of HBM per device.

```python
import math
import jax
import jax.numpy as jnp
import numpy as np
from jax import lax

D = 7168
EXPERTS = 256
TOP = 8
FF = 1024
TOK_DEV = 128
CAP = 6
TOKENS = 1024
LIVE = 8
N_EXP = 8


def block_scale(own_key, dims, cuts, least, top_value):
    factor_of = 1.0
    for dim, parts in cuts:
        heights = jax.random.uniform(jax.random.fold_in(jax.random.fold_in(own_key, 6), dim), (parts,), jnp.float32, least / len(cuts), top_value / len(cuts))
        factor_of = factor_of * jnp.repeat(jnp.exp(heights), dims[dim] // parts).reshape((-1,) + (1,) * (len(dims) - 1 - dim))
    return factor_of


def assign_block(key, own, number, rows, count, top, most, slope):
    ranking = jax.random.permutation(key, count)
    crowded, common = shares(count, rows * top, most, slope, True), shares(count, rows * top, most, slope, False)
    places = jnp.arange(count)

    def named(sizes, offset_by):
        used = int((sizes > 0).sum())
        fixed = max(1, used // 4)
        passed = fixed + (places - fixed + offset_by * (used - fixed)) % max(1, count - fixed)
        return jnp.zeros((count,), jnp.int32).at[ranking[jnp.where(places < fixed, places, passed)]].set(jnp.asarray(sizes, jnp.int32))

    sizes = jnp.where(number % 4 == 0, named(crowded, number // 4), named(common, number - number // 4 - 1))
    mixed = jax.random.permutation(jax.random.fold_in(own, 3), count)
    donor, taker = mixed[0:count // 2 * 2:2], mixed[1:count // 2 * 2:2]
    room = jnp.minimum(sizes[donor] - 1, most - sizes[taker]) // 2
    room = jnp.where((donor == ranking[0]) | (taker == ranking[0]) | (sizes[taker] == 0), 0, jnp.maximum(room, 0))
    passed = jax.random.randint(jax.random.fold_in(own, 4), (count // 2,), 0, 1 << 20) % (room + 1)
    sizes = sizes.at[donor].add(-passed).at[taker].add(passed)
    items = jnp.searchsorted(jnp.cumsum(sizes), jnp.arange(rows * top), side="right").astype(jnp.int32)
    listing = items.reshape(top, rows).T
    listing = listing[jax.random.permutation(jax.random.fold_in(own, 1), rows)]
    offset_by = jax.random.randint(jax.random.fold_in(own, 2), (rows, 1), 0, top)
    return jnp.take_along_axis(listing, (jnp.arange(top)[None, :] + offset_by) % top, axis=1)


def shares(number_of, total, bound, skew, full):
    portions = [(1 << 20) // math.isqrt(rank ** skew) + 1 for rank in range(1, number_of + 1)]
    largest = bound if full else min(bound, max(-(-total // number_of), total * portions[0] // sum(portions)))
    least = 1 if total - largest >= number_of - 1 else 0
    holding, surplus = [largest] + [least] * (number_of - 1), total - largest - least * (number_of - 1)
    while surplus > 0:
        movable = [i for i in range(1, number_of) if holding[i] < largest] or [i for i in range(1, number_of) if holding[i] < bound]
        mass, budget = sum([portions[i] for i in movable]), surplus
        for i in movable:
            extra = min(bound - holding[i], max(1, budget * portions[i] // mass), surplus)
            holding[i] = holding[i] + extra
            surplus = surplus - extra
    return np.array(holding)


def bell_draw(stream_key, shape, spread, most, pieces=(), kind=jnp.bfloat16):
    result = spread * jax.random.normal(stream_key, shape, jnp.float32)
    if pieces:
        result = result * block_scale(stream_key, shape, pieces, -0.22, 0.18)
    return jnp.clip(result, -most, most).astype(kind)


def setup_inputs(seed: int = 0) -> dict:
    seeds = jax.random.split(jax.random.key(seed), 8)
    tokens = bell_draw(seeds[0], (TOKENS, D), 1.0, 6.0, ((0, 8), (1, 4)))
    cotangent = bell_draw(seeds[1], (TOKENS, D), 1.0, 6.0, ((0, 8), (1, 4)))
    routes_keys = jax.random.split(jax.random.fold_in(seeds[2], 1), TOKENS // TOK_DEV)
    routes_turns = jax.random.permutation(jax.random.fold_in(seeds[2], 3), TOKENS // TOK_DEV)
    routes = jax.vmap(lambda own, number: assign_block(jax.random.fold_in(seeds[2], 2), own, number, TOK_DEV, EXPERTS, TOP, CAP, 2))(routes_keys, routes_turns).reshape((TOKENS, TOP))
    gate_weights = jnp.clip(0.1 + 0.59999999 * jax.random.uniform(seeds[3], (TOKENS, TOP), jnp.float32) ** block_scale(seeds[3], (TOKENS, TOP), ((0, 8),), -0.2, 0.2), 0.1, 0.7)
    w_gate = bell_draw(seeds[4], (LIVE, D, FF), D ** -0.5, 0.0625, ((0, 8), (1, 4)))
    w_up = bell_draw(seeds[5], (LIVE, D, FF), D ** -0.5, 0.0625, ((0, 8), (1, 4)))
    w_down = bell_draw(seeds[6], (LIVE, FF, D), FF ** -0.5, 0.1875, ((0, 8), (2, 4)))
    return dict(tokens=tokens, cotangent=cotangent, routes=routes, gate_weights=gate_weights, w_gate=w_gate, w_up=w_up, w_down=w_down)


def expert_pass(inputs):
    rows, grads, gate_matrix, up_matrix, down_matrix = inputs
    gate = jnp.dot(rows, gate_matrix, preferred_element_type=jnp.float32)
    up = jnp.dot(rows, up_matrix, preferred_element_type=jnp.float32)
    back = jnp.dot(grads, down_matrix.T, preferred_element_type=jnp.float32)
    sigmoid_gate = jax.nn.sigmoid(gate)
    activated = gate * sigmoid_gate
    hidden = (activated * up).astype(jnp.bfloat16)
    d_gate_act = (back * up * sigmoid_gate * (1.0 + gate * (1.0 - sigmoid_gate))).astype(jnp.bfloat16)
    d_up_act = (back * activated).astype(jnp.bfloat16)
    expert_out = jnp.dot(hidden, down_matrix, preferred_element_type=jnp.float32).astype(jnp.bfloat16)
    d_down = jnp.dot(hidden.T, grads, preferred_element_type=jnp.float32).astype(jnp.bfloat16)
    d_gate = jnp.dot(rows.T, d_gate_act, preferred_element_type=jnp.float32).astype(jnp.bfloat16)
    d_up = jnp.dot(rows.T, d_up_act, preferred_element_type=jnp.float32).astype(jnp.bfloat16)
    d_rows = (jnp.dot(d_gate_act, gate_matrix.T, preferred_element_type=jnp.float32)
              + jnp.dot(d_up_act, up_matrix.T, preferred_element_type=jnp.float32)).astype(jnp.bfloat16)
    return expert_out, d_rows, d_gate, d_up, d_down


def to_experts(slot_array):
    shaped = slot_array.reshape(N_EXP, N_EXP, CAP, slot_array.shape[-1])
    return jnp.transpose(shaped, (1, 0, 2, 3)).reshape(N_EXP, N_EXP * CAP, slot_array.shape[-1])


def from_experts(expert_array):
    shaped = expert_array.reshape(N_EXP, N_EXP, CAP, expert_array.shape[-1])
    return jnp.transpose(shaped, (1, 0, 2, 3)).reshape(N_EXP, N_EXP * CAP, expert_array.shape[-1])


def reference(tokens, cotangent, routes, gate_weights, w_gate, w_up, w_down):
    pair_count = TOK_DEV * TOP
    block_ids = routes.reshape(N_EXP, pair_count)
    columns = jnp.arange(N_EXP, dtype=jnp.int32)
    onehot = (block_ids[:, :, None] == columns[None, None, :]).astype(jnp.int32)
    earlier = jnp.cumsum(onehot, axis=1) - onehot
    slot_index = jnp.sum(onehot * earlier, axis=2).astype(jnp.int32)
    target = jnp.where(block_ids < N_EXP, block_ids * CAP + slot_index, -1).astype(jnp.int32)
    places = jnp.arange(N_EXP * CAP, dtype=jnp.int32)
    matches = target[:, None, :] == places[None, :, None]
    present = jnp.any(matches, axis=2)
    positions = jnp.arange(pair_count, dtype=jnp.int32)
    where_at = jnp.sum(jnp.where(matches, positions[None, None, :], 0), axis=2).astype(jnp.int32)
    block_start = (jnp.arange(N_EXP, dtype=jnp.int32) * TOK_DEV)[:, None]
    token_index = (block_start + where_at // TOP).astype(jnp.int32)
    pick_index = (where_at % TOP).astype(jnp.int32)
    rounded = gate_weights.astype(jnp.bfloat16).astype(jnp.float32)
    slot_gate = jnp.where(present, rounded[token_index, pick_index], 0.0)
    slot_rows = jnp.where(present[:, :, None], tokens[token_index], 0).astype(jnp.bfloat16)
    slot_grads = (slot_gate[:, :, None] * cotangent[token_index].astype(jnp.float32)).astype(jnp.bfloat16)
    results = lax.map(expert_pass, (to_experts(slot_rows), to_experts(slot_grads), w_gate, w_up, w_down))
    expert_out, d_rows, d_gate, d_up, d_down = results
    out_slots = from_experts(expert_out).astype(jnp.float32)
    grad_slots = from_experts(d_rows).astype(jnp.float32)
    flat_index = token_index.reshape(-1)
    combined = jax.ops.segment_sum((slot_gate[:, :, None] * out_slots).reshape(-1, D), flat_index, num_segments=TOKENS)
    d_tokens = jax.ops.segment_sum(jnp.where(present[:, :, None], grad_slots, 0.0).reshape(-1, D), flat_index, num_segments=TOKENS)
    return combined.astype(jnp.bfloat16), d_tokens.astype(jnp.bfloat16), d_gate, d_up, d_down
```

```python
import functools

import jax
import jax.numpy as jnp
from jax import lax
from jax.experimental import pallas as pl
from jax.experimental.pallas import tpu as pltpu
from jax.sharding import PartitionSpec as P

HALF = 8
PAIR = 2 * HALF


def dot(left, right, left_dim=1, right_dim=0):
    return lax.dot_general(
        left,
        right,
        (((left_dim,), (right_dim,)), ((), ())),
        preferred_element_type=jnp.float32,
    )


def pieces(width):
    if width % 256 or width < 512:
        return [(0, width)]
    first = (width // 256 + 1) // 2 * 256
    return [(0, first), (first, width - first)]


def selections(routes, gates, count):
    tok_count, picks = routes.shape
    shape = (tok_count, count * PAIR)
    lane = lax.broadcasted_iota(jnp.int32, shape, 1)
    expert = lane // PAIR
    second = (lane % PAIR) >= HALF
    slot = (lane % HALF).astype(jnp.float32)
    gates = gates.astype(jnp.bfloat16).astype(jnp.float32)
    named = jnp.zeros(shape, jnp.float32)
    weight = jnp.zeros(shape, jnp.float32)
    for k in range(picks):
        match = routes[:, k : k + 1] == expert
        named = jnp.where(match, 1.0, named)
        weight = jnp.where(match, gates[:, k : k + 1], weight)
    square = (tok_count, tok_count)
    before = lax.broadcasted_iota(jnp.int32, square, 1) < lax.broadcasted_iota(
        jnp.int32, square, 0
    )
    earlier = dot(jnp.where(before, 1.0, 0.0).astype(jnp.bfloat16), named.astype(jnp.bfloat16))
    hit = jnp.where(earlier == slot, named, 0.0)
    select = jnp.where(second, 0.0, hit).astype(jnp.bfloat16)
    weighting = jnp.where(second, hit * weight, 0.0).astype(jnp.bfloat16)
    return select, weighting


def exchange_kernel(
    n_ctx, n_exp, tokens, cotangent, routes, gates, w_gate_hbm, w_up_hbm, w_down_hbm,
    slots_out, acts_out, back_out, select_out, weighting_out,
    w_gate, w_up, w_down, send, got, total, part, arrived, acts, back_send, back,
    load_sem, out_send, out_recv, sum_send, sum_recv, act_send, act_recv, ret_send, ret_recv,
):
    my_ctx, my_exp = lax.axis_index("ctx"), lax.axis_index("exp")
    width = tokens.shape[1]
    ff = w_gate.shape[1]
    rows = n_exp * HALF
    share = rows // n_ctx
    cuts = pieces(width)

    barrier = pltpu.get_barrier_semaphore()
    for d in range(1, n_exp):
        pl.semaphore_signal(
            barrier, inc=1, device_id=(my_ctx, lax.rem(my_exp + d, n_exp)),
            device_id_type=pl.DeviceIdType.MESH,
        )
    for d in range(1, n_ctx):
        pl.semaphore_signal(
            barrier, inc=1, device_id=(lax.rem(my_ctx + d, n_ctx), my_exp),
            device_id_type=pl.DeviceIdType.MESH,
        )
    loads = [
        pltpu.make_async_copy(src, dst, load_sem.at[i])
        for i, (src, dst) in enumerate(
            ((w_gate_hbm, w_gate), (w_up_hbm, w_up), (w_down_hbm, w_down))
        )
    ]
    for load in loads:
        load.start()

    select, weighting = selections(routes[...], gates[...], n_exp)
    select_out[...] = select
    weighting_out[...] = weighting
    pl.semaphore_wait(barrier, n_exp - 1 + n_ctx - 1)

    def scatter(c, src, dst, send_sem, recv_sem):
        start, size = cuts[c]
        copies = []
        for d in range(1, n_exp):
            peer = lax.rem(my_exp + d, n_exp)
            copy = pltpu.make_async_remote_copy(
                src_ref=src.at[pl.ds(pl.multiple_of(peer * PAIR, PAIR), PAIR), pl.ds(start, size)],
                dst_ref=dst.at[pl.ds(pl.multiple_of(my_exp * PAIR, PAIR), PAIR), pl.ds(start, size)],
                send_sem=send_sem.at[c, d],
                recv_sem=recv_sem.at[c, d],
                device_id=(my_ctx, peer),
                device_id_type=pl.DeviceIdType.MESH,
            )
            copy.start()
            copies.append(copy)
        own = pl.ds(pl.multiple_of(my_exp * PAIR, PAIR), PAIR)
        dst[own, pl.ds(start, size)] = src[own, pl.ds(start, size)]
        return copies

    out_copies = []
    for c, (start, size) in enumerate(cuts):
        cols = pl.ds(start, size)
        send[:, cols] = (
            dot(select, tokens[:, cols], 0, 0) + dot(weighting, cotangent[:, cols], 0, 0)
        ).astype(jnp.bfloat16)
        out_copies.append(scatter(c, send, got, out_send, out_recv))

    my_rows = pl.ds(pl.multiple_of(my_ctx * share, share), share)

    def share_out(index):
        copies = []
        for d in range(1, n_ctx):
            peer = lax.rem(my_ctx + d, n_ctx)
            copy = pltpu.make_async_remote_copy(
                src_ref=part.at[index, pl.ds(pl.multiple_of(peer * share, share), share)],
                dst_ref=arrived.at[index, d],
                send_sem=sum_send.at[index, d],
                recv_sem=sum_recv.at[index, d],
                device_id=(peer, my_exp),
                device_id_type=pl.DeviceIdType.MESH,
            )
            copy.start()
            copies.append(copy)
        return copies

    sum_copies = []
    for c, (start, size) in enumerate(cuts):
        cols = pl.ds(start, size)
        for copy in out_copies[c]:
            copy.wait_recv()
        for index in range(3):
            if c == 0:
                loads[index].wait()
            if index == 0:
                result = dot(got[:, cols], w_gate[cols, :])
            elif index == 1:
                result = dot(got[:, cols], w_up[cols, :])
            else:
                result = dot(got[:, cols], w_down[:, cols], 1, 1)
            result = result.reshape(n_exp, 2, HALF, ff)[:, index // 2].reshape(rows, ff)
            if c:
                result = total[index] + result
            total[index] = result
            if c == len(cuts) - 1:
                part[index] = result.astype(jnp.bfloat16)
                sum_copies.append(share_out(index))
    slots_out[...] = got[...]

    def summed(index):
        result = total[index, my_rows]
        for d in range(1, n_ctx):
            sum_copies[index][d - 1].wait_recv()
            result = result + arrived[index, d].astype(jnp.float32)
        return result

    def gather(index):
        copies = []
        for d in range(1, n_ctx):
            copy = pltpu.make_async_remote_copy(
                src_ref=acts.at[index, my_rows],
                dst_ref=acts.at[index, my_rows],
                send_sem=act_send.at[index, d],
                recv_sem=act_recv.at[index, d],
                device_id=(lax.rem(my_ctx + d, n_ctx), my_exp),
                device_id_type=pl.DeviceIdType.MESH,
            )
            copy.start()
            copies.append(copy)
        return copies

    gate, up = summed(0), summed(1)
    sigmoid = jax.nn.sigmoid(gate)
    activated = gate * sigmoid
    acts[0, my_rows] = (activated * up).astype(jnp.bfloat16)
    act_copies = [gather(0)]
    grad = summed(2)
    acts[1, my_rows] = (grad * up * sigmoid * (1.0 + gate * (1.0 - sigmoid))).astype(jnp.bfloat16)
    act_copies.append(gather(1))
    acts[2, my_rows] = (grad * activated).astype(jnp.bfloat16)
    act_copies.append(gather(2))

    spread = []
    for index in range(3):
        for copy in act_copies[index]:
            copy.wait_recv()
        value = acts[index].astype(jnp.float32).reshape(n_exp, 1, HALF, ff)
        empty = jnp.zeros_like(value)
        both = (empty, value) if index == 0 else (value, empty)
        value = jnp.concatenate(both, axis=1).reshape(n_exp * PAIR, ff).astype(jnp.bfloat16)
        acts_out[index] = value
        spread.append(value)

    ret_copies = []
    for c, (start, size) in enumerate(cuts):
        cols = pl.ds(start, size)
        back_send[:, cols] = (
            dot(spread[0], w_down[:, cols])
            + dot(spread[1], w_gate[cols, :], 1, 1)
            + dot(spread[2], w_up[cols, :], 1, 1)
        ).astype(jnp.bfloat16)
        ret_copies.append(scatter(c, back_send, back, ret_send, ret_recv))
    for c, (start, size) in enumerate(cuts):
        cols = pl.ds(start, size)
        for copy in ret_copies[c]:
            copy.wait_recv()
        back_out[:, cols] = back[:, cols]
    for copies in out_copies + sum_copies + act_copies + ret_copies:
        for copy in copies:
            copy.wait_send()


def gradient_kernel(slots, acts, back, select, weighting, combined, d_tokens, d_gate, d_up, d_down):
    combined[...] = dot(weighting[...], back[...]).astype(jnp.bfloat16)
    d_tokens[...] = dot(select[...], back[...]).astype(jnp.bfloat16)
    d_gate[0] = dot(slots[...], acts[1], 0, 0).astype(jnp.bfloat16)
    d_up[0] = dot(slots[...], acts[2], 0, 0).astype(jnp.bfloat16)
    d_down[0] = dot(acts[0], slots[...], 0, 0).astype(jnp.bfloat16)


def shards(tokens, cotangent, routes, gate_weights, w_gate, w_up, w_down):
    n_ctx, n_exp = lax.axis_size("ctx"), lax.axis_size("exp")
    tok_count, width = tokens.shape
    ff = w_gate.shape[2]
    rows, packed = n_exp * HALF, n_exp * PAIR
    share = rows // n_ctx
    cuts = len(pieces(width))
    bf16, f32 = jnp.bfloat16, jnp.float32
    vmem = pl.BlockSpec(memory_space=pltpu.VMEM)
    hbm = pl.BlockSpec(memory_space=pl.ANY)
    dma = pltpu.SemaphoreType.DMA
    slots, acts, back, select, weighting = pl.pallas_call(
        functools.partial(exchange_kernel, n_ctx, n_exp),
        out_shape=(
            jax.ShapeDtypeStruct((packed, width), bf16),
            jax.ShapeDtypeStruct((3, packed, ff), bf16),
            jax.ShapeDtypeStruct((packed, width), bf16),
            jax.ShapeDtypeStruct((tok_count, packed), bf16),
            jax.ShapeDtypeStruct((tok_count, packed), bf16),
        ),
        in_specs=[vmem] * 4 + [hbm] * 3,
        out_specs=(vmem,) * 5,
        scratch_shapes=[
            pltpu.VMEM((width, ff), bf16),
            pltpu.VMEM((width, ff), bf16),
            pltpu.VMEM((ff, width), bf16),
            pltpu.VMEM((packed, width), bf16),
            pltpu.VMEM((packed, width), bf16),
            pltpu.VMEM((3, rows, ff), f32),
            pltpu.VMEM((3, rows, ff), bf16),
            pltpu.VMEM((3, n_ctx, share, ff), bf16),
            pltpu.VMEM((3, rows, ff), bf16),
            pltpu.VMEM((packed, width), bf16),
            pltpu.VMEM((packed, width), bf16),
            dma((3,)),
            dma((cuts, n_exp)),
            dma((cuts, n_exp)),
            dma((3, n_ctx)),
            dma((3, n_ctx)),
            dma((3, n_ctx)),
            dma((3, n_ctx)),
            dma((cuts, n_exp)),
            dma((cuts, n_exp)),
        ],
        compiler_params=pltpu.CompilerParams(
            collective_id=0, has_side_effects=True, vmem_limit_bytes=44 * 2**20
        ),
    )(tokens, cotangent, routes, gate_weights, w_gate[0], w_up[0], w_down[0])

    block = 256 if width % 256 == 0 else width
    whole = lambda *shape: pl.BlockSpec(shape, lambda i: (0,) * len(shape))
    return pl.pallas_call(
        gradient_kernel,
        grid=(width // block,),
        out_shape=(
            jax.ShapeDtypeStruct((tok_count, width), bf16),
            jax.ShapeDtypeStruct((tok_count, width), bf16),
            jax.ShapeDtypeStruct((1, width, ff), bf16),
            jax.ShapeDtypeStruct((1, width, ff), bf16),
            jax.ShapeDtypeStruct((1, ff, width), bf16),
        ),
        in_specs=[
            pl.BlockSpec((packed, block), lambda i: (0, i)),
            whole(3, packed, ff),
            pl.BlockSpec((packed, block), lambda i: (0, i)),
            whole(tok_count, packed),
            whole(tok_count, packed),
        ],
        out_specs=(
            pl.BlockSpec((tok_count, block), lambda i: (0, i)),
            pl.BlockSpec((tok_count, block), lambda i: (0, i)),
            pl.BlockSpec((1, block, ff), lambda i: (0, i, 0)),
            pl.BlockSpec((1, block, ff), lambda i: (0, i, 0)),
            pl.BlockSpec((1, ff, block), lambda i: (0, 0, i)),
        ),
        compiler_params=pltpu.CompilerParams(vmem_limit_bytes=32 * 2**20),
    )(slots, acts, back, select, weighting)


def solution(mesh):
    in_specs = (
        P("exp", "ctx"),
        P("exp", "ctx"),
        P("exp", None),
        P("exp", None),
        P("exp", "ctx", None),
        P("exp", "ctx", None),
        P("exp", None, "ctx"),
    )
    out_specs = (
        P("exp", "ctx"),
        P("exp", "ctx"),
        P("exp", "ctx", None),
        P("exp", "ctx", None),
        P("exp", None, "ctx"),
    )
    return jax.shard_map(shards, mesh=mesh, in_specs=in_specs, out_specs=out_specs, check_vma=False)
```

```python
import functools

import jax
import jax.numpy as jnp
from jax import lax
from jax.experimental import pallas as pl
from jax.experimental.pallas import tpu as pltpu
from jax.sharding import PartitionSpec as P

HALF = 8
PAIR = 2 * HALF


def dot(left, right, left_dim=1, right_dim=0):
    return lax.dot_general(
        left,
        right,
        (((left_dim,), (right_dim,)), ((), ())),
        preferred_element_type=jnp.float32,
    )


def halves(width):
    first = -(-width // 256) * 128
    return (0, first), (first, width - first)


def widen(value, width):
    if value.shape[1] == width:
        return value
    rest = jnp.zeros((value.shape[0], width - value.shape[1]), value.dtype)
    return jnp.concatenate([value, rest], axis=1)


def selections(routes, gates, count):
    picks, tok_count = routes.shape
    shape = (count * PAIR, tok_count)
    line = lax.broadcasted_iota(jnp.int32, shape, 0)
    expert = line // PAIR
    second = (line % PAIR) >= HALF
    slot = (line % HALF).astype(jnp.float32)
    gates = gates.astype(jnp.bfloat16).astype(jnp.float32)
    named = jnp.zeros(shape, jnp.float32)
    weight = jnp.zeros(shape, jnp.float32)
    for k in range(picks):
        match = routes[k : k + 1, :] == expert
        named = jnp.where(match, 1.0, named)
        weight = jnp.where(match, gates[k : k + 1, :], weight)
    square = (tok_count, tok_count)
    before = lax.broadcasted_iota(jnp.int32, square, 0) < lax.broadcasted_iota(
        jnp.int32, square, 1
    )
    earlier = dot(named.astype(jnp.bfloat16), jnp.where(before, 1.0, 0.0).astype(jnp.bfloat16))
    hit = jnp.where(earlier == slot, named, 0.0)
    weight = hit * weight
    return [
        jnp.where(second == later, value, 0.0).astype(jnp.bfloat16)
        for value in (hit, weight)
        for later in (False, True)
    ]


def exchange_kernel(
    n_ctx, n_exp, routes, gates, tokens_hbm, cotangent_hbm, w_gate_hbm, w_up_hbm, w_down_hbm,
    slots_out, acts_out, back_out, select_out,
    tokens, cotangent, w_gate, w_up, w_down, send, got, total, part, arrived, acts, back_send, back,
    load_sem, out_send, out_recv, sum_send, sum_recv, act_send, act_recv, ret_send, ret_recv,
):
    my_ctx, my_exp = lax.axis_index("ctx"), lax.axis_index("exp")
    width = tokens.shape[1]
    ff = w_gate.shape[1]
    rows = n_exp * HALF
    share = rows // n_ctx
    left, right = halves(width)
    left, right, half = pl.ds(*left), pl.ds(*right), left[1]

    barrier = pltpu.get_barrier_semaphore()
    for d in range(1, n_exp):
        pl.semaphore_signal(
            barrier, inc=1, device_id=(my_ctx, lax.rem(my_exp + d, n_exp)),
            device_id_type=pl.DeviceIdType.MESH,
        )
    for d in range(1, n_ctx):
        pl.semaphore_signal(
            barrier, inc=1, device_id=(lax.rem(my_ctx + d, n_ctx), my_exp),
            device_id_type=pl.DeviceIdType.MESH,
        )
    loads = [
        pltpu.make_async_copy(src, dst, load_sem.at[i])
        for i, (src, dst) in enumerate(
            (
                (tokens_hbm, tokens),
                (cotangent_hbm, cotangent),
                (w_gate_hbm, w_gate),
                (w_up_hbm, w_up),
                (w_down_hbm, w_down),
            )
        )
    ]
    for load in loads:
        load.start()

    chosen = selections(routes[...], gates[...], n_exp)

    def scatter(kind, src, dst, send_sem, recv_sem):
        copies = []
        mine = pl.ds(pl.multiple_of(my_exp * PAIR, PAIR), PAIR)
        for d in range(1, n_exp):
            peer = lax.rem(my_exp + d, n_exp)
            copy = pltpu.make_async_remote_copy(
                src_ref=src.at[kind, pl.ds(pl.multiple_of(peer * PAIR, PAIR), PAIR)],
                dst_ref=dst.at[kind, mine],
                send_sem=send_sem.at[kind, d],
                recv_sem=recv_sem.at[kind, d],
                device_id=(my_ctx, peer),
                device_id_type=pl.DeviceIdType.MESH,
            )
            copy.start()
            copies.append(copy)
        dst[kind, mine] = src[kind, mine]
        return copies

    out_copies = []
    for kind, data in enumerate((tokens, cotangent)):
        loads[kind].wait()
        send[kind] = (
            dot(chosen[2 * kind], data[:, left])
            + widen(dot(chosen[2 * kind + 1], data[:, right]), half)
        ).astype(jnp.bfloat16)
        if kind == 0:
            pl.semaphore_wait(barrier, n_exp - 1 + n_ctx - 1)
        out_copies.append(scatter(kind, send, got, out_send, out_recv))
    for i in range(4):
        select_out[i] = chosen[i]

    my_rows = pl.ds(pl.multiple_of(my_ctx * share, share), share)

    def share_out(index):
        copies = []
        for d in range(1, n_ctx):
            peer = lax.rem(my_ctx + d, n_ctx)
            copy = pltpu.make_async_remote_copy(
                src_ref=part.at[index, pl.ds(pl.multiple_of(peer * share, share), share)],
                dst_ref=arrived.at[index, d],
                send_sem=sum_send.at[index, d],
                recv_sem=sum_recv.at[index, d],
                device_id=(peer, my_exp),
                device_id_type=pl.DeviceIdType.MESH,
            )
            copy.start()
            copies.append(copy)
        return copies

    def pick(value, which):
        return value.reshape(n_exp, 2, HALF, ff)[:, which].reshape(rows, ff)

    sum_copies = []
    for index in range(3):
        kind = index // 2
        if index != 1:
            for copy in out_copies[kind]:
                copy.wait_recv()
        loads[2 + index].wait()
        rest = pl.ds(0, right.size)
        if index < 2:
            weights = w_gate if index == 0 else w_up
            first = dot(got[kind], weights[left, :])
            second = dot(got[kind, :, rest], weights[right, :])
        else:
            first = dot(got[kind], w_down[:, left], 1, 1)
            second = dot(got[kind, :, rest], w_down[:, right], 1, 1)
        result = pick(first, 0) + pick(second, 1)
        total[index] = result
        part[index] = result.astype(jnp.bfloat16)
        sum_copies.append(share_out(index))
    slots_out[...] = got[...]

    def summed(index):
        result = total[index, my_rows]
        for d in range(1, n_ctx):
            sum_copies[index][d - 1].wait_recv()
            result = result + arrived[index, d].astype(jnp.float32)
        return result

    def gather(index):
        copies = []
        for d in range(1, n_ctx):
            copy = pltpu.make_async_remote_copy(
                src_ref=acts.at[index, my_rows],
                dst_ref=acts.at[index, my_rows],
                send_sem=act_send.at[index, d],
                recv_sem=act_recv.at[index, d],
                device_id=(lax.rem(my_ctx + d, n_ctx), my_exp),
                device_id_type=pl.DeviceIdType.MESH,
            )
            copy.start()
            copies.append(copy)
        return copies

    gate, up = summed(0), summed(1)
    sigmoid = jax.nn.sigmoid(gate)
    activated = gate * sigmoid
    acts[0, my_rows] = (activated * up).astype(jnp.bfloat16)
    act_copies = [gather(0)]
    grad = summed(2)
    acts[1, my_rows] = (grad * up * sigmoid * (1.0 + gate * (1.0 - sigmoid))).astype(jnp.bfloat16)
    act_copies.append(gather(1))
    acts[2, my_rows] = (grad * activated).astype(jnp.bfloat16)
    act_copies.append(gather(2))

    def pack(first, second):
        both = [first, widen(second, half)]
        both = [value.reshape(n_exp, 1, HALF, half) for value in both]
        return jnp.concatenate(both, axis=1).reshape(n_exp * PAIR, half).astype(jnp.bfloat16)

    for copy in act_copies[0]:
        copy.wait_recv()
    back_send[0] = pack(dot(acts[0], w_down[:, left]), dot(acts[0], w_down[:, right]))
    ret_copies = [scatter(0, back_send, back, ret_send, ret_recv)]
    for copy in act_copies[1] + act_copies[2]:
        copy.wait_recv()
    back_send[1] = pack(
        dot(acts[1], w_gate[left, :], 1, 1) + dot(acts[2], w_up[left, :], 1, 1),
        dot(acts[1], w_gate[right, :], 1, 1) + dot(acts[2], w_up[right, :], 1, 1),
    )
    ret_copies.append(scatter(1, back_send, back, ret_send, ret_recv))
    acts_out[...] = acts[...]
    for kind in range(2):
        for copy in ret_copies[kind]:
            copy.wait_recv()
        back_out[kind] = back[kind]
    for copies in out_copies + sum_copies + act_copies + ret_copies:
        for copy in copies:
            copy.wait_send()


def gradient_kernel(
    n_exp, slots, acts, back, select, combined_hbm, d_tokens_hbm, d_gate_hbm, d_up_hbm, d_down_hbm,
    combined, d_tokens, d_gate, d_up, d_down, sems,
):
    width, ff = d_gate.shape
    rows = n_exp * HALF
    cuts = halves(width)
    copies = []

    def store(src, dst):
        copy = pltpu.make_async_copy(src, dst, sems.at[len(copies)])
        copy.start()
        copies.append(copy)

    def unpack(kind):
        value = slots[kind].astype(jnp.float32).reshape(n_exp, 2, HALF, -1)
        return [
            value[:, i].reshape(rows, -1)[:, :size].astype(jnp.bfloat16)
            for i, (_, size) in enumerate(cuts)
        ]

    row_halves = unpack(0)
    for i, (start, size) in enumerate(cuts):
        at = pl.ds(start, size)
        for index, buf, hbm in ((1, d_gate, d_gate_hbm), (2, d_up, d_up_hbm)):
            buf[at, :] = dot(row_halves[i], acts[index], 0, 0).astype(jnp.bfloat16)
            store(buf.at[at], hbm.at[at])
    grad_halves = unpack(1)
    for lo in range(0, ff, ff // 2):
        at = pl.ds(lo, ff // 2)
        for i, (start, size) in enumerate(cuts):
            d_down[at, pl.ds(start, size)] = dot(acts[0, :, at], grad_halves[i], 0, 0).astype(
                jnp.bfloat16
            )
        store(d_down.at[at], d_down_hbm.at[at])
    for kind, buf, hbm in ((0, combined, combined_hbm), (1, d_tokens, d_tokens_hbm)):
        for i, (start, size) in enumerate(cuts):
            matrix = select[2 * (1 - kind) + i]
            buf[:, pl.ds(start, size)] = dot(matrix, back[kind, :, pl.ds(0, size)], 0, 0).astype(
                jnp.bfloat16
            )
        store(buf, hbm)
    for copy in copies:
        copy.wait()


def shards(tokens, cotangent, routes, gate_weights, w_gate, w_up, w_down):
    n_ctx, n_exp = lax.axis_size("ctx"), lax.axis_size("exp")
    tok_count, width = tokens.shape
    ff = w_gate.shape[2]
    rows, packed = n_exp * HALF, n_exp * PAIR
    share = rows // n_ctx
    half = halves(width)[0][1]
    bf16, f32 = jnp.bfloat16, jnp.float32
    vmem = pl.BlockSpec(memory_space=pltpu.VMEM)
    hbm = pl.BlockSpec(memory_space=pltpu.HBM)
    dma = pltpu.SemaphoreType.DMA
    slots, acts, back, select = pl.pallas_call(
        functools.partial(exchange_kernel, n_ctx, n_exp),
        out_shape=(
            jax.ShapeDtypeStruct((2, packed, half), bf16),
            jax.ShapeDtypeStruct((3, rows, ff), bf16),
            jax.ShapeDtypeStruct((2, packed, half), bf16),
            jax.ShapeDtypeStruct((4, packed, tok_count), bf16),
        ),
        in_specs=[vmem] * 2 + [hbm] * 5,
        out_specs=(vmem,) * 4,
        scratch_shapes=[
            pltpu.VMEM((tok_count, width), bf16),
            pltpu.VMEM((tok_count, width), bf16),
            pltpu.VMEM((width, ff), bf16),
            pltpu.VMEM((width, ff), bf16),
            pltpu.VMEM((ff, width), bf16),
            pltpu.VMEM((2, packed, half), bf16),
            pltpu.VMEM((2, packed, half), bf16),
            pltpu.VMEM((3, rows, ff), f32),
            pltpu.VMEM((3, rows, ff), bf16),
            pltpu.VMEM((3, n_ctx, share, ff), bf16),
            pltpu.VMEM((3, rows, ff), bf16),
            pltpu.VMEM((2, packed, half), bf16),
            pltpu.VMEM((2, packed, half), bf16),
            dma((5,)),
            dma((2, n_exp)),
            dma((2, n_exp)),
            dma((3, n_ctx)),
            dma((3, n_ctx)),
            dma((3, n_ctx)),
            dma((3, n_ctx)),
            dma((2, n_exp)),
            dma((2, n_exp)),
        ],
        compiler_params=pltpu.CompilerParams(
            collective_id=0, has_side_effects=True, vmem_limit_bytes=60 * 2**20
        ),
    )(routes.T, gate_weights.T, tokens, cotangent, w_gate[0], w_up[0], w_down[0])

    combined, d_tokens, d_gate, d_up, d_down = pl.pallas_call(
        functools.partial(gradient_kernel, n_exp),
        out_shape=(
            jax.ShapeDtypeStruct((tok_count, width), bf16),
            jax.ShapeDtypeStruct((tok_count, width), bf16),
            jax.ShapeDtypeStruct((width, ff), bf16),
            jax.ShapeDtypeStruct((width, ff), bf16),
            jax.ShapeDtypeStruct((ff, width), bf16),
        ),
        in_specs=[vmem] * 4,
        out_specs=(hbm,) * 5,
        scratch_shapes=[
            pltpu.VMEM((tok_count, width), bf16),
            pltpu.VMEM((tok_count, width), bf16),
            pltpu.VMEM((width, ff), bf16),
            pltpu.VMEM((width, ff), bf16),
            pltpu.VMEM((ff, width), bf16),
            dma((8,)),
        ],
        compiler_params=pltpu.CompilerParams(vmem_limit_bytes=44 * 2**20),
    )(slots, acts, back, select)
    return combined, d_tokens, d_gate[None], d_up[None], d_down[None]


def solution(mesh):
    in_specs = (
        P("exp", "ctx"),
        P("exp", "ctx"),
        P("exp", None),
        P("exp", None),
        P("exp", "ctx", None),
        P("exp", "ctx", None),
        P("exp", None, "ctx"),
    )
    out_specs = (
        P("exp", "ctx"),
        P("exp", "ctx"),
        P("exp", "ctx", None),
        P("exp", "ctx", None),
        P("exp", None, "ctx"),
    )
    return jax.shard_map(shards, mesh=mesh, in_specs=in_specs, out_specs=out_specs, check_vma=False)
```

```python
import functools

import jax
import jax.numpy as jnp
from jax import lax
from jax.experimental import pallas as pl
from jax.experimental.pallas import tpu as pltpu
from jax.sharding import PartitionSpec as P

HALF = 8
PAIR = 2 * HALF


def dot(left, right, left_dim=1, right_dim=0):
    return lax.dot_general(
        left,
        right,
        (((left_dim,), (right_dim,)), ((), ())),
        preferred_element_type=jnp.float32,
    )


def halves(width):
    first = -(-width // 256) * 128
    return (0, first), (first, width - first)


def widen(value, width):
    if value.shape[1] == width:
        return value
    rest = jnp.zeros((value.shape[0], width - value.shape[1]), value.dtype)
    return jnp.concatenate([value, rest], axis=1)


def selections(routes, gates, count):
    picks, tok_count = routes.shape
    shape = (count * PAIR, tok_count)
    line = lax.broadcasted_iota(jnp.int32, shape, 0)
    expert = line // PAIR
    second = (line % PAIR) >= HALF
    slot = (line % HALF).astype(jnp.float32)
    gates = gates.astype(jnp.bfloat16).astype(jnp.float32)
    named = jnp.zeros(shape, jnp.float32)
    weight = jnp.zeros(shape, jnp.float32)
    for k in range(picks):
        match = routes[k : k + 1, :] == expert
        named = jnp.where(match, 1.0, named)
        weight = jnp.where(match, gates[k : k + 1, :], weight)
    square = (tok_count, tok_count)
    before = lax.broadcasted_iota(jnp.int32, square, 0) < lax.broadcasted_iota(
        jnp.int32, square, 1
    )
    earlier = dot(named.astype(jnp.bfloat16), jnp.where(before, 1.0, 0.0).astype(jnp.bfloat16))
    hit = jnp.where(earlier == slot, named, 0.0)
    weight = hit * weight
    return [
        jnp.where(second == later, value, 0.0).astype(jnp.bfloat16)
        for value in (hit, weight)
        for later in (False, True)
    ]


def exchange_kernel(
    n_ctx, n_exp, routes, gates, tokens_hbm, cotangent_hbm, w_gate_hbm, w_up_hbm, w_down_hbm,
    slots_out, acts_out, back_out, select_out,
    tokens, cotangent, w_gate, w_up, w_down, select, send, got, total, part, arrived, acts, back_send,
    back, load_sem, store_sem, out_send, out_recv, sum_send, sum_recv, act_send, act_recv, ret_send, ret_recv,
):
    my_ctx, my_exp = lax.axis_index("ctx"), lax.axis_index("exp")
    width = tokens.shape[1]
    ff = w_gate.shape[1]
    rows = n_exp * HALF
    share = rows // n_ctx
    left, right = halves(width)
    left, right, half = pl.ds(*left), pl.ds(*right), left[1]

    barrier = pltpu.get_barrier_semaphore()
    for d in range(1, n_exp):
        pl.semaphore_signal(
            barrier, inc=1, device_id=(my_ctx, lax.rem(my_exp + d, n_exp)),
            device_id_type=pl.DeviceIdType.MESH,
        )
    for d in range(1, n_ctx):
        pl.semaphore_signal(
            barrier, inc=1, device_id=(lax.rem(my_ctx + d, n_ctx), my_exp),
            device_id_type=pl.DeviceIdType.MESH,
        )
    loads = [
        pltpu.make_async_copy(src, dst, load_sem.at[i])
        for i, (src, dst) in enumerate(
            (
                (tokens_hbm, tokens),
                (cotangent_hbm, cotangent),
                (w_gate_hbm, w_gate),
                (w_up_hbm, w_up),
                (w_down_hbm, w_down),
            )
        )
    ]
    for load in loads:
        load.start()

    chosen = selections(routes[...], gates[...], n_exp)

    def scatter(kind, src, dst, send_sem, recv_sem):
        copies = []
        mine = pl.ds(pl.multiple_of(my_exp * PAIR, PAIR), PAIR)
        for d in range(1, n_exp):
            peer = lax.rem(my_exp + d, n_exp)
            copy = pltpu.make_async_remote_copy(
                src_ref=src.at[kind, pl.ds(pl.multiple_of(peer * PAIR, PAIR), PAIR)],
                dst_ref=dst.at[kind, mine],
                send_sem=send_sem.at[kind, d],
                recv_sem=recv_sem.at[kind, d],
                device_id=(my_ctx, peer),
                device_id_type=pl.DeviceIdType.MESH,
            )
            copy.start()
            copies.append(copy)
        dst[kind, mine] = src[kind, mine]
        return copies

    out_copies = []
    for kind, data in enumerate((tokens, cotangent)):
        loads[kind].wait()
        send[kind] = (
            dot(chosen[2 * kind], data[:, left])
            + widen(dot(chosen[2 * kind + 1], data[:, right]), half)
        ).astype(jnp.bfloat16)
        if kind == 0:
            pl.semaphore_wait(barrier, n_exp - 1 + n_ctx - 1)
        out_copies.append(scatter(kind, send, got, out_send, out_recv))
    stores = []

    def store(src, dst):
        copy = pltpu.make_async_copy(src, dst, store_sem.at[len(stores)])
        copy.start()
        stores.append(copy)

    for i in range(4):
        select[i] = chosen[i]
    store(select, select_out)

    my_rows = pl.ds(pl.multiple_of(my_ctx * share, share), share)

    def share_out(index):
        copies = []
        for d in range(1, n_ctx):
            peer = lax.rem(my_ctx + d, n_ctx)
            copy = pltpu.make_async_remote_copy(
                src_ref=part.at[index, pl.ds(pl.multiple_of(peer * share, share), share)],
                dst_ref=arrived.at[index, d],
                send_sem=sum_send.at[index, d],
                recv_sem=sum_recv.at[index, d],
                device_id=(peer, my_exp),
                device_id_type=pl.DeviceIdType.MESH,
            )
            copy.start()
            copies.append(copy)
        return copies

    def pick(value, which):
        return value.reshape(n_exp, 2, HALF, ff)[:, which].reshape(rows, ff)

    sum_copies = []
    for index in range(3):
        kind = index // 2
        if index != 1:
            for copy in out_copies[kind]:
                copy.wait_recv()
        loads[2 + index].wait()
        rest = pl.ds(0, right.size)
        if index < 2:
            weights = w_gate if index == 0 else w_up
            first = dot(got[kind], weights[left, :])
            second = dot(got[kind, :, rest], weights[right, :])
        else:
            first = dot(got[kind], w_down[:, left], 1, 1)
            second = dot(got[kind, :, rest], w_down[:, right], 1, 1)
        result = pick(first, 0) + pick(second, 1)
        total[index] = result
        part[index] = result.astype(jnp.bfloat16)
        sum_copies.append(share_out(index))
    store(got, slots_out)

    def summed(index):
        result = total[index, my_rows]
        for d in range(1, n_ctx):
            sum_copies[index][d - 1].wait_recv()
            result = result + arrived[index, d].astype(jnp.float32)
        return result

    def gather(index):
        copies = []
        for d in range(1, n_ctx):
            copy = pltpu.make_async_remote_copy(
                src_ref=acts.at[index, my_rows],
                dst_ref=acts.at[index, my_rows],
                send_sem=act_send.at[index, d],
                recv_sem=act_recv.at[index, d],
                device_id=(lax.rem(my_ctx + d, n_ctx), my_exp),
                device_id_type=pl.DeviceIdType.MESH,
            )
            copy.start()
            copies.append(copy)
        return copies

    gate, up = summed(0), summed(1)
    sigmoid = jax.nn.sigmoid(gate)
    activated = gate * sigmoid
    acts[0, my_rows] = (activated * up).astype(jnp.bfloat16)
    act_copies = [gather(0)]
    grad = summed(2)
    acts[1, my_rows] = (grad * up * sigmoid * (1.0 + gate * (1.0 - sigmoid))).astype(jnp.bfloat16)
    act_copies.append(gather(1))
    acts[2, my_rows] = (grad * activated).astype(jnp.bfloat16)
    act_copies.append(gather(2))

    def pack(first, second):
        both = [first, widen(second, half)]
        both = [value.reshape(n_exp, 1, HALF, half) for value in both]
        return jnp.concatenate(both, axis=1).reshape(n_exp * PAIR, half).astype(jnp.bfloat16)

    for copy in act_copies[0]:
        copy.wait_recv()
    back_send[0] = pack(dot(acts[0], w_down[:, left]), dot(acts[0], w_down[:, right]))
    ret_copies = [scatter(0, back_send, back, ret_send, ret_recv)]
    for copy in act_copies[1]:
        copy.wait_recv()
    first, second = dot(acts[1], w_gate[left, :], 1, 1), dot(acts[1], w_gate[right, :], 1, 1)
    for copy in act_copies[2]:
        copy.wait_recv()
    back_send[1] = pack(
        first + dot(acts[2], w_up[left, :], 1, 1),
        second + dot(acts[2], w_up[right, :], 1, 1),
    )
    ret_copies.append(scatter(1, back_send, back, ret_send, ret_recv))
    store(acts, acts_out)
    for kind in range(2):
        for copy in ret_copies[kind]:
            copy.wait_recv()
        store(back.at[kind], back_out.at[kind])
    for copies in out_copies + sum_copies + act_copies + ret_copies:
        for copy in copies:
            copy.wait_send()
    for copy in stores:
        copy.wait()


def gradient_kernel(
    n_exp, slots_hbm, acts_hbm, back_hbm, select_hbm,
    combined_hbm, d_tokens_hbm, d_gate_hbm, d_up_hbm, d_down_hbm,
    slots, acts, back, select, combined, d_tokens, d_gate, d_up, d_down, load_sem, sems,
):
    loads = [
        pltpu.make_async_copy(src, dst, load_sem.at[i])
        for i, (src, dst) in enumerate(
            ((slots_hbm, slots), (acts_hbm, acts), (back_hbm, back), (select_hbm, select))
        )
    ]
    for load in loads:
        load.start()
    width, ff = d_gate.shape
    rows = n_exp * HALF
    cuts = halves(width)
    copies = []

    def store(src, dst):
        copy = pltpu.make_async_copy(src, dst, sems.at[len(copies)])
        copy.start()
        copies.append(copy)

    def unpack(kind):
        value = slots[kind].astype(jnp.float32).reshape(n_exp, 2, HALF, -1)
        return [
            value[:, i].reshape(rows, -1)[:, :size].astype(jnp.bfloat16)
            for i, (_, size) in enumerate(cuts)
        ]

    loads[0].wait()
    row_halves = unpack(0)
    loads[1].wait()
    for i, (start, size) in enumerate(cuts):
        at = pl.ds(start, size)
        for index, buf, hbm in ((1, d_gate, d_gate_hbm), (2, d_up, d_up_hbm)):
            buf[at, :] = dot(row_halves[i], acts[index], 0, 0).astype(jnp.bfloat16)
            store(buf.at[at], hbm.at[at])
    grad_halves = unpack(1)
    for lo in range(0, ff, ff // 2):
        at = pl.ds(lo, ff // 2)
        for i, (start, size) in enumerate(cuts):
            d_down[at, pl.ds(start, size)] = dot(acts[0, :, at], grad_halves[i], 0, 0).astype(
                jnp.bfloat16
            )
        store(d_down.at[at], d_down_hbm.at[at])
    loads[2].wait()
    loads[3].wait()
    for kind, buf, hbm in ((0, combined, combined_hbm), (1, d_tokens, d_tokens_hbm)):
        for i, (start, size) in enumerate(cuts):
            matrix = select[2 * (1 - kind) + i]
            buf[:, pl.ds(start, size)] = dot(matrix, back[kind, :, pl.ds(0, size)], 0, 0).astype(
                jnp.bfloat16
            )
        store(buf, hbm)
    for copy in copies:
        copy.wait()


def shards(tokens, cotangent, routes, gate_weights, w_gate, w_up, w_down):
    n_ctx, n_exp = lax.axis_size("ctx"), lax.axis_size("exp")
    tok_count, width = tokens.shape
    ff = w_gate.shape[2]
    rows, packed = n_exp * HALF, n_exp * PAIR
    share = rows // n_ctx
    half = halves(width)[0][1]
    bf16, f32 = jnp.bfloat16, jnp.float32
    vmem = pl.BlockSpec(memory_space=pltpu.VMEM)
    hbm = pl.BlockSpec(memory_space=pltpu.HBM)
    dma = pltpu.SemaphoreType.DMA
    slots, acts, back, select = pl.pallas_call(
        functools.partial(exchange_kernel, n_ctx, n_exp),
        out_shape=(
            jax.ShapeDtypeStruct((2, packed, half), bf16),
            jax.ShapeDtypeStruct((3, rows, ff), bf16),
            jax.ShapeDtypeStruct((2, packed, half), bf16),
            jax.ShapeDtypeStruct((4, packed, tok_count), bf16),
        ),
        in_specs=[vmem] * 2 + [hbm] * 5,
        out_specs=(hbm,) * 4,
        scratch_shapes=[
            pltpu.VMEM((tok_count, width), bf16),
            pltpu.VMEM((tok_count, width), bf16),
            pltpu.VMEM((width, ff), bf16),
            pltpu.VMEM((width, ff), bf16),
            pltpu.VMEM((ff, width), bf16),
            pltpu.VMEM((4, packed, tok_count), bf16),
            pltpu.VMEM((2, packed, half), bf16),
            pltpu.VMEM((2, packed, half), bf16),
            pltpu.VMEM((3, rows, ff), f32),
            pltpu.VMEM((3, rows, ff), bf16),
            pltpu.VMEM((3, n_ctx, share, ff), bf16),
            pltpu.VMEM((3, rows, ff), bf16),
            pltpu.VMEM((2, packed, half), bf16),
            pltpu.VMEM((2, packed, half), bf16),
            dma((5,)),
            dma((5,)),
            dma((2, n_exp)),
            dma((2, n_exp)),
            dma((3, n_ctx)),
            dma((3, n_ctx)),
            dma((3, n_ctx)),
            dma((3, n_ctx)),
            dma((2, n_exp)),
            dma((2, n_exp)),
        ],
        compiler_params=pltpu.CompilerParams(
            collective_id=0, has_side_effects=True, vmem_limit_bytes=60 * 2**20
        ),
    )(routes.T, gate_weights.T, tokens, cotangent, w_gate[0], w_up[0], w_down[0])

    combined, d_tokens, d_gate, d_up, d_down = pl.pallas_call(
        functools.partial(gradient_kernel, n_exp),
        out_shape=(
            jax.ShapeDtypeStruct((tok_count, width), bf16),
            jax.ShapeDtypeStruct((tok_count, width), bf16),
            jax.ShapeDtypeStruct((width, ff), bf16),
            jax.ShapeDtypeStruct((width, ff), bf16),
            jax.ShapeDtypeStruct((ff, width), bf16),
        ),
        in_specs=[hbm] * 4,
        out_specs=(hbm,) * 5,
        scratch_shapes=[
            pltpu.VMEM((2, packed, half), bf16),
            pltpu.VMEM((3, rows, ff), bf16),
            pltpu.VMEM((2, packed, half), bf16),
            pltpu.VMEM((4, packed, tok_count), bf16),
            pltpu.VMEM((tok_count, width), bf16),
            pltpu.VMEM((tok_count, width), bf16),
            pltpu.VMEM((width, ff), bf16),
            pltpu.VMEM((width, ff), bf16),
            pltpu.VMEM((ff, width), bf16),
            dma((4,)),
            dma((8,)),
        ],
        compiler_params=pltpu.CompilerParams(vmem_limit_bytes=60 * 2**20),
    )(slots, acts, back, select)
    return combined, d_tokens, d_gate[None], d_up[None], d_down[None]


def solution(mesh):
    in_specs = (
        P("exp", "ctx"),
        P("exp", "ctx"),
        P("exp", None),
        P("exp", None),
        P("exp", "ctx", None),
        P("exp", "ctx", None),
        P("exp", None, "ctx"),
    )
    out_specs = (
        P("exp", "ctx"),
        P("exp", "ctx"),
        P("exp", "ctx", None),
        P("exp", "ctx", None),
        P("exp", None, "ctx"),
    )
    return jax.shard_map(shards, mesh=mesh, in_specs=in_specs, out_specs=out_specs, check_vma=False)
```
